128 devices in a mesh: wide: 32 (over y, z_lo, x), narrow: 4 (over z_hi, core).
Axes of the slice: x: 4, y: 4, z: 4 (z_hi: 2, z_lo: 2; z = z_hi * 2 + z_lo), core: 2. Of those that a mesh axis runs over, the one named last changes fastest.
Arguments:
- tokens: bfloat16 [65536, 1024], P(('wide', 'narrow')), may hold values from -6 to 6
- router: bfloat16 [1024, 256], replicated, may hold values from -3 to 3
- expert_in: bfloat16 [128, 1024, 2048], P(('wide', 'narrow')), may hold values from -0.1875 to 0.1875
- expert_out: bfloat16 [128, 2048, 1024], P(('wide', 'narrow')), may hold values from -0.125 to 0.125
- upstream: bfloat16 [65536, 1024], P(('wide', 'narrow')), may hold values from -6 to 6
Outputs:
- token_grad: bfloat16 [65536, 1024], P(('wide', 'narrow'))
- router_grad: float32 [1024, 256], replicated
- expert_in_grad: bfloat16 [128, 1024, 2048], P(('wide', 'narrow'))
- expert_out_grad: bfloat16 [128, 2048, 1024], P(('wide', 'narrow'))
The draws below stay inside these ranges and needn't reach their ends.
All inputs are finite; a program needn't handle non-finite values.
Results may differ from the reference program's by a relative error of at most 0.0089.
Values may be sent and summed in bfloat16 or wider, within the bound.
A program may use at most 128 MiB of HBM per device.

```python
import math
import jax
import jax.numpy as jnp
from jax import lax

D = 1024
FF = 2048
M = 256
P_SIZE = 2
E = 128
S = 256
TOKENS = 65536


def token_base(key):
    base_key = jax.random.fold_in(key, 11)
    return jnp.clip(jax.random.normal(base_key, (TOKENS, D), jnp.float32), -6.0, 6.0)


def draw_tokens(key, part):
    base_rows = token_base(key)
    return base_rows.astype(jnp.bfloat16)


def draw_router(key, part):
    own_key = jax.random.fold_in(key, 3)
    router = 3.0 * jnp.clip(jax.random.normal(own_key, (D, S), jnp.float32), -6.0, 6.0) / math.sqrt(D)
    return router.astype(jnp.bfloat16)


def shard_levels(key, extent, cuts, least, high):
    def one(position, shards_of):
        draws = jax.random.uniform(jax.random.fold_in(jax.random.fold_in(key, 6), position), (shards_of,), jnp.float32, least / len(cuts), high / len(cuts))
        return jnp.repeat(jnp.exp(draws), extent[position] // shards_of).reshape((-1,) + (1,) * (len(extent) - position - 1))

    level = one(*cuts[0])
    for cut in cuts[1:]:
        level = level * one(*cut)
    return level


def scatter_about(key, shape, width, limit, split=(), kind=jnp.bfloat16):
    values = jax.random.normal(key, shape, jnp.float32) * width
    if len(split) > 0:
        values = shard_levels(key, shape, split, -0.22, 0.18) * values
    return jnp.clip(values, min=-limit, max=limit).astype(kind)


def setup_inputs(seed: int = 0) -> dict:
    key_list = jax.random.split(jax.random.key(seed), 6)
    return {
        "tokens": draw_tokens(jax.random.fold_in(key_list[5], 71), 0),
        "router": draw_router(jax.random.fold_in(key_list[5], 71), 0),
        "expert_in": scatter_about(key_list[2], (E, D, FF), D ** -0.5, 0.1875, ((0, 128),)),
        "expert_out": scatter_about(key_list[3], (E, FF, D), FF ** -0.5, 0.125, ((0, 128),)),
        "upstream": scatter_about(key_list[4], (TOKENS, D), 1.0, 6.0, ((0, 128),)),
    }


root_two_pi = math.sqrt(2.0 / math.pi)
cubic_coef = 0.044715

def gelu_value(hidden):
    return 0.5 * hidden * (1.0 + jnp.tanh(root_two_pi * (hidden + cubic_coef * hidden ** 3)))

def gelu_slope(hidden):
    tangent = jnp.tanh(root_two_pi * (hidden + cubic_coef * hidden ** 3))
    return 0.5 * (1.0 + tangent) + 0.5 * hidden * (1.0 - tangent * tangent) * root_two_pi * (1.0 + 3.0 * cubic_coef * hidden * hidden)

def expert_step(pieces):
    rows_in, rows_grad, first_weight, second_weight = pieces
    hidden = jnp.dot(rows_in, first_weight, preferred_element_type=jnp.float32)
    active = gelu_value(hidden).astype(jnp.bfloat16)
    outputs = jnp.dot(active, second_weight, preferred_element_type=jnp.float32).astype(jnp.bfloat16)
    active_grad = jnp.dot(rows_grad, second_weight.T, preferred_element_type=jnp.float32)
    second_grad = jnp.dot(active.T, rows_grad, preferred_element_type=jnp.float32).astype(jnp.bfloat16)
    pre_grad = (active_grad * gelu_slope(hidden)).astype(jnp.bfloat16)
    first_grad = jnp.dot(rows_in.T, pre_grad, preferred_element_type=jnp.float32).astype(jnp.bfloat16)
    slot_back = jnp.dot(pre_grad, first_weight.T, preferred_element_type=jnp.float32).astype(jnp.bfloat16)
    return (outputs, slot_back, first_grad, second_grad)

def reference(tokens, router, expert_in, expert_out, upstream):
    images = TOKENS // M
    tokens3 = tokens.reshape(images, M, D).astype(jnp.float32)
    upstream3 = upstream.reshape(images, M, D).astype(jnp.float32)
    router32 = router.astype(jnp.float32)
    logits = jnp.einsum('imd,ds->ims', tokens3, router32)
    dispatch = jax.nn.softmax(logits, axis=1)
    combine = jax.nn.softmax(logits, axis=2)
    dispatch_low = dispatch.astype(jnp.bfloat16).astype(jnp.float32)
    combine_low = combine.astype(jnp.bfloat16).astype(jnp.float32)
    slot_in = jnp.einsum('ims,imd->isd', dispatch_low, tokens3).astype(jnp.bfloat16)
    slot_grad = jnp.einsum('ims,imd->isd', combine_low, upstream3).astype(jnp.bfloat16)

    def by_expert(array):
        return array.reshape(images, E, P_SIZE, D).transpose(1, 0, 2, 3).reshape(E, images * P_SIZE, D)

    def by_image(array):
        return array.reshape(E, images, P_SIZE, D).transpose(1, 0, 2, 3).reshape(images, S, D)
    outputs, slot_back, first_grad, second_grad = lax.map(expert_step, (by_expert(slot_in), by_expert(slot_grad), expert_in, expert_out))
    slot_out = by_image(outputs).astype(jnp.float32)
    slot_back = by_image(slot_back).astype(jnp.float32)
    dispatch_grad = jnp.einsum('imd,isd->ims', tokens3, slot_back)
    combine_grad = jnp.einsum('imd,isd->ims', upstream3, slot_out)
    logit_grad = dispatch * (dispatch_grad - lax.optimization_barrier(jnp.sum(dispatch * dispatch_grad, axis=1, keepdims=True)))
    logit_grad = logit_grad + combine * (combine_grad - lax.optimization_barrier(jnp.sum(combine * combine_grad, axis=2, keepdims=True)))
    logit_low = logit_grad.astype(jnp.bfloat16).astype(jnp.float32)
    token_grad = jnp.einsum('ims,isd->imd', dispatch_low, slot_back) + jnp.einsum('ims,ds->imd', logit_low, router32)
    token_grad = token_grad.astype(jnp.bfloat16).reshape(TOKENS, D)
    router_grad = jnp.einsum('imd,ims->ds', tokens3, logit_low)
    return (token_grad, router_grad, first_grad, second_grad)
```

```python
import math

import jax
import jax.numpy as jnp
from jax import lax
from jax.sharding import PartitionSpec as P

M = 256
P_SIZE = 2


root_two_pi = math.sqrt(2.0 / math.pi)
cubic_coef = 0.044715


def gelu_value(hidden):
    return 0.5 * hidden * (1.0 + jnp.tanh(root_two_pi * (hidden + cubic_coef * hidden**3)))


def gelu_slope(hidden):
    tangent = jnp.tanh(root_two_pi * (hidden + cubic_coef * hidden**3))
    return 0.5 * (1.0 + tangent) + 0.5 * hidden * (1.0 - tangent * tangent) * root_two_pi * (
        1.0 + 3.0 * cubic_coef * hidden * hidden
    )


def send_inputs(array):
    return lax.all_to_all(array, ("wide", "narrow"), split_axis=0, concat_axis=0, tiled=True)


def send_outputs(array):
    return lax.all_to_all(array, ("wide", "narrow"), split_axis=0, concat_axis=0, tiled=True)


def send_grads(array):
    return lax.all_to_all(array, ("wide", "narrow"), split_axis=0, concat_axis=0, tiled=True)


def send_returns(array):
    return lax.all_to_all(array, ("wide", "narrow"), split_axis=0, concat_axis=0, tiled=True)


def expert_forward(rows_in, first_weight, second_weight):
    hidden = jnp.dot(rows_in, first_weight, preferred_element_type=jnp.float32)
    active = gelu_value(hidden).astype(jnp.bfloat16)
    outputs = jnp.dot(active, second_weight, preferred_element_type=jnp.float32).astype(
        jnp.bfloat16
    )
    return (hidden, active, outputs)


def expert_backward(rows_in, rows_grad, hidden, active, first_weight, second_weight):
    active_grad = jnp.einsum(
        "rd,fd->rf", rows_grad, second_weight, preferred_element_type=jnp.float32
    )
    second_grad = jnp.einsum(
        "rf,rd->fd", active, rows_grad, preferred_element_type=jnp.float32
    ).astype(jnp.bfloat16)
    pre_grad = (active_grad * gelu_slope(hidden)).astype(jnp.bfloat16)
    first_grad = jnp.einsum(
        "rd,rf->df", rows_in, pre_grad, preferred_element_type=jnp.float32
    ).astype(jnp.bfloat16)
    slot_back = jnp.einsum(
        "rf,df->rd", pre_grad, first_weight, preferred_element_type=jnp.float32
    ).astype(jnp.bfloat16)
    return (first_grad, second_grad, slot_back)


def local(tokens, router, expert_in, expert_out, upstream):
    wide_count = lax.axis_size("wide")
    narrow_count = lax.axis_size("narrow")
    experts = wide_count * narrow_count
    images = tokens.shape[0] // M
    model_width = tokens.shape[1]
    slot_count = router.shape[1]
    tokens3 = tokens.reshape(images, M, model_width)
    upstream3 = upstream.reshape(images, M, model_width)
    logits = jnp.einsum("imd,ds->ims", tokens3, router, preferred_element_type=jnp.float32)
    dispatch = jax.nn.softmax(logits, axis=1)
    combine = jax.nn.softmax(logits, axis=2)
    dispatch_low = dispatch.astype(jnp.bfloat16).reshape(images, M, experts, P_SIZE)
    combine_low = combine.astype(jnp.bfloat16).reshape(images, M, experts, P_SIZE)
    slot_shape = (experts, images * P_SIZE, model_width)
    slot_in = (
        jnp.einsum("imep,imd->eipd", dispatch_low, tokens3, preferred_element_type=jnp.float32)
        .astype(jnp.bfloat16)
        .reshape(slot_shape)
    )
    slot_grad = (
        jnp.einsum("imep,imd->eipd", combine_low, upstream3, preferred_element_type=jnp.float32)
        .astype(jnp.bfloat16)
        .reshape(slot_shape)
    )
    first_weight = expert_in[0]
    second_weight = expert_out[0]
    rows_in = send_inputs(slot_in).reshape(-1, model_width)
    hidden, active, outputs = expert_forward(rows_in, first_weight, second_weight)
    slot_out = send_outputs(outputs.reshape(slot_shape))
    rows_grad = send_grads(slot_grad).reshape(-1, model_width)
    first_grad, second_grad, slot_back = expert_backward(
        rows_in, rows_grad, hidden, active, first_weight, second_weight
    )
    slot_return = send_returns(slot_back.reshape(slot_shape))
    out_four = slot_out.reshape(experts, images, P_SIZE, model_width)
    return_four = slot_return.reshape(experts, images, P_SIZE, model_width)
    dispatch_grad = jnp.einsum(
        "imd,eipd->imep", tokens3, return_four, preferred_element_type=jnp.float32
    ).reshape(images, M, slot_count)
    combine_grad = jnp.einsum(
        "imd,eipd->imep", upstream3, out_four, preferred_element_type=jnp.float32
    ).reshape(images, M, slot_count)
    logit_grad = dispatch * (
        dispatch_grad - jnp.sum(dispatch * dispatch_grad, axis=1, keepdims=True)
    )
    logit_grad = logit_grad + combine * (
        combine_grad - jnp.sum(combine * combine_grad, axis=2, keepdims=True)
    )
    logit_low = logit_grad.astype(jnp.bfloat16)
    token_grad = jnp.einsum(
        "imep,eipd->imd", dispatch_low, return_four, preferred_element_type=jnp.float32
    )
    token_grad = token_grad + jnp.einsum(
        "ims,ds->imd", logit_low, router, preferred_element_type=jnp.float32
    )
    token_grad = token_grad.astype(jnp.bfloat16).reshape(-1, model_width)
    router_part = jnp.einsum("ims,imd->sd", logit_low, tokens3, preferred_element_type=jnp.float32)
    terms = send_inputs(router_part.astype(jnp.bfloat16).reshape(experts, P_SIZE, model_width))
    own_rows = jnp.sum(terms.astype(jnp.float32), axis=0).astype(jnp.bfloat16)
    rows = lax.all_gather(own_rows, ("wide", "narrow"), axis=0, tiled=True)
    router_grad = rows.T.astype(jnp.float32)
    return (token_grad, router_grad, first_grad[None], second_grad[None])


def solution(mesh):
    return jax.shard_map(
        local,
        mesh=mesh,
        in_specs=(
            P(("wide", "narrow"), None),
            P(),
            P(("wide", "narrow"), None, None),
            P(("wide", "narrow"), None, None),
            P(("wide", "narrow"), None),
        ),
        out_specs=(
            P(("wide", "narrow"), None),
            P(),
            P(("wide", "narrow"), None, None),
            P(("wide", "narrow"), None, None),
        ),
        check_vma=False,
    )
```

```python
import math

import jax
import jax.numpy as jnp
from jax import lax
from jax.experimental import pallas as pl
from jax.experimental.pallas import tpu as pltpu
from jax.sharding import PartitionSpec as P

MESH = pl.DeviceIdType.MESH
F32 = jnp.float32
BF16 = jnp.bfloat16
N = 128
WIDTH = 1024
FF = 2048
M = 256
SLOTS = 256
ROWS = 8
GROUP = 32
GROUPS = N // GROUP
CHUNK = GROUP * ROWS
HALF = CHUNK // 2
FTILE = 512
STRIDE = 37

root_two_pi = math.sqrt(2.0 / math.pi)
cubic_coef = 0.044715


def dot(a, b, ca=1, cb=0):
    return lax.dot_general(a, b, (((ca,), (cb,)), ((), ())), preferred_element_type=F32)


def kernel(
    tokens_hbm,
    router_hbm,
    first_hbm,
    second_hbm,
    upstream_hbm,
    token_grad_hbm,
    router_grad_hbm,
    first_grad_hbm,
    second_grad_hbm,
    tokens,
    router,
    first,
    second,
    upstream,
    router_rel,
    turn,
    interleave,
    dispatch,
    combine,
    parts,
    send_buf,
    recv_buf,
    rows_in,
    rows_grad,
    active,
    pre_grad,
    out_acc,
    back_acc,
    back_buf,
    return_buf,
    first_grad,
    second_grad,
    token_grad,
    logit_abs,
    terms,
    terms_in,
    own_sum,
    gathered,
    router_grad,
    load_sem,
    store_sem,
    send_sem,
    recv_sem,
    back_send_sem,
    back_recv_sem,
    term_sem,
    gather_sem,
):
    me = lax.axis_index("wide") * 4 + lax.axis_index("narrow")

    def device(number):
        return (number // 4, number % 4)

    def ahead(k):
        return (me + STRIDE * k) % N

    def behind(k):
        return (me + (N - STRIDE) * k) % N

    loads = [
        pltpu.make_async_copy(src, dst, load_sem.at[n])
        for n, (src, dst) in enumerate(
            (
                (router_hbm, router),
                (tokens_hbm, tokens),
                (upstream_hbm, upstream),
                (first_hbm.at[0], first),
                (second_hbm.at[0], second),
            )
        )
    ]
    for load in loads:
        load.start()

    barrier = pltpu.get_barrier_semaphore()

    def greet(k, carry):
        pl.semaphore_signal(barrier, inc=1, device_id=device((me + k) % N), device_id_type=MESH)
        return carry

    lax.fori_loop(1, N, greet, 0)

    row = lax.broadcasted_iota(jnp.int32, (SLOTS, SLOTS), 0)
    col = lax.broadcasted_iota(jnp.int32, (SLOTS, SLOTS), 1)
    slot = 2 * ((me + STRIDE * (col >> 1)) & (N - 1)) + (col & 1)
    turn[...] = jnp.where(row == slot, 1.0, 0.0).astype(BF16)
    row = lax.broadcasted_iota(jnp.int32, (CHUNK, CHUNK), 0)
    col = lax.broadcasted_iota(jnp.int32, (CHUNK, CHUNK), 1)
    origin = ((row >> 1) & 3) * (2 * GROUP) + 2 * (row >> 3) + (row & 1)
    interleave[...] = jnp.where(col == origin, 1.0, 0.0).astype(BF16)

    loads[0].wait()
    router_rel[...] = dot(router[...], turn[...]).astype(BF16)
    loads[1].wait()
    loads[2].wait()
    for i in range(2):
        image = pl.ds(M * i, M)
        logits = dot(tokens[image, :], router_rel[...])
        top = jnp.exp(logits - jnp.max(logits, axis=0, keepdims=True))
        disp = top / jnp.sum(top, axis=0, keepdims=True)
        top = jnp.exp(logits - jnp.max(logits, axis=1, keepdims=True))
        comb = top / jnp.sum(top, axis=1, keepdims=True)
        dispatch[image, :] = disp
        combine[image, :] = comb
        parts[i] = dot(disp.astype(BF16), tokens[image, :], 0, 0).astype(BF16)
        parts[2 + i] = dot(comb.astype(BF16), upstream[image, :], 0, 0).astype(BF16)

    pl.semaphore_wait(barrier, N - 1)

    def send_copy(k):
        return pltpu.make_async_remote_copy(
            src_ref=send_buf.at[k],
            dst_ref=recv_buf.at[k],
            send_sem=send_sem,
            recv_sem=recv_sem.at[k // GROUP],
            device_id=device(ahead(k)),
            device_id_type=MESH,
        )

    own = pltpu.make_async_copy(send_buf.at[0], recv_buf.at[0], recv_sem.at[0])
    for g in range(GROUPS):
        stack = parts[:, 2 * GROUP * g : 2 * GROUP * (g + 1), :].reshape(CHUNK, WIDTH)
        send_buf[GROUP * g : GROUP * (g + 1)] = (
            dot(interleave[...], stack).astype(BF16).reshape(GROUP, ROWS, WIDTH)
        )
        if g == 0:
            own.start()

        def send(k, carry):
            send_copy(k).start()
            return carry

        lax.fori_loop(max(1, GROUP * g), GROUP * (g + 1), send, 0)

    loads[3].wait()
    loads[4].wait()

    def back_copy(k):
        return pltpu.make_async_remote_copy(
            src_ref=back_buf.at[k],
            dst_ref=return_buf.at[k],
            send_sem=back_send_sem,
            recv_sem=back_recv_sem,
            device_id=device(behind(k)),
            device_id_type=MESH,
        )

    def expert(g, carry):
        group = pl.ds(pl.multiple_of(g * GROUP, GROUP), GROUP)
        rows = pl.ds(pl.multiple_of(g * HALF, HALF), HALF)
        pltpu.make_async_copy(recv_buf.at[group], recv_buf.at[group], recv_sem.at[g]).wait()
        split = dot(interleave[...], recv_buf[group].reshape(CHUNK, WIDTH), 0, 0).astype(BF16)
        rows_in[rows, :] = split[:HALF]
        rows_grad[rows, :] = split[HALF:]
        out_acc[...] = jnp.zeros_like(out_acc)
        back_acc[...] = jnp.zeros_like(back_acc)

        def tile(t, inner):
            cols = pl.ds(pl.multiple_of(t * FTILE, FTILE), FTILE)
            hidden = dot(rows_in[rows, :], first[:, cols])
            grad = dot(rows_grad[rows, :], second[cols, :], 1, 1)
            square = hidden * hidden
            tangent = jnp.tanh(root_two_pi * (hidden + cubic_coef * square * hidden))
            act = (0.5 * hidden * (1.0 + tangent)).astype(BF16)
            slope = 0.5 * (1.0 + tangent) + 0.5 * hidden * (1.0 - tangent * tangent) * root_two_pi * (
                1.0 + 3.0 * cubic_coef * square
            )
            pre = (grad * slope).astype(BF16)
            active[rows, cols] = act
            pre_grad[rows, cols] = pre
            out_acc[...] += dot(act, second[cols, :])
            back_acc[...] += dot(pre, first[:, cols], 1, 1)
            return inner

        lax.fori_loop(0, FF // FTILE, tile, 0)
        both = jnp.concatenate([out_acc[...].astype(BF16), back_acc[...].astype(BF16)], axis=0)
        back_buf[group] = dot(interleave[...], both).astype(BF16).reshape(GROUP, ROWS, WIDTH)

        @pl.when(g == 0)
        def _():
            pltpu.make_async_copy(back_buf.at[0], return_buf.at[0], back_recv_sem).start()

        def send(k, inner):
            back_copy(k).start()
            return inner

        lax.fori_loop(jnp.maximum(1, GROUP * g), GROUP * (g + 1), send, 0)
        return carry

    lax.fori_loop(0, GROUPS, expert, 0)

    def weights(t, carry):
        cols = pl.ds(pl.multiple_of(t * FTILE, FTILE), FTILE)
        second_grad[cols, :] = dot(active[:, cols], rows_grad[...], 0, 0).astype(BF16)
        first_grad[:, cols] = dot(rows_in[...], pre_grad[:, cols], 0, 0).astype(BF16)
        return carry

    lax.fori_loop(0, FF // FTILE, weights, 0)
    stores = [
        pltpu.make_async_copy(src, dst, store_sem.at[n])
        for n, (src, dst) in enumerate(
            (
                (first_grad, first_grad_hbm.at[0]),
                (second_grad, second_grad_hbm.at[0]),
                (token_grad, token_grad_hbm),
                (router_grad, router_grad_hbm),
            )
        )
    ]
    stores[0].start()
    stores[1].start()

    pltpu.make_async_copy(return_buf, return_buf, back_recv_sem).wait()
    for g in range(GROUPS):
        chunk = return_buf[GROUP * g : GROUP * (g + 1)].reshape(CHUNK, WIDTH)
        split = dot(interleave[...], chunk, 0, 0).astype(BF16)
        parts[:, 2 * GROUP * g : 2 * GROUP * (g + 1), :] = split.reshape(4, 2 * GROUP, WIDTH)
    lows = []
    for i in range(2):
        image = pl.ds(M * i, M)
        disp = dispatch[image, :]
        comb = combine[image, :]
        combine_grad = dot(upstream[image, :], parts[i], 1, 1)
        dispatch_grad = dot(tokens[image, :], parts[2 + i], 1, 1)
        logit_grad = disp * (dispatch_grad - jnp.sum(disp * dispatch_grad, axis=0, keepdims=True))
        logit_grad = logit_grad + comb * (
            combine_grad - jnp.sum(comb * combine_grad, axis=1, keepdims=True)
        )
        low = logit_grad.astype(BF16)
        lows.append(low)
        logit_abs[image, :] = dot(low, turn[...], 1, 1).astype(BF16)
    total = dot(tokens[...], logit_abs[...], 0, 0).astype(BF16)
    terms[0] = total[:, :128]
    terms[1] = total[:, 128:]

    def block(ref, number):
        return ref.at[number % 2, pl.ds(pl.multiple_of((number // 2) * 16, 16), 16), :]

    pltpu.make_async_copy(block(terms, me), terms_in.at[0], term_sem.at[1]).start()

    def send_term(k, carry):
        pltpu.make_async_remote_copy(
            src_ref=block(terms, ahead(k)),
            dst_ref=terms_in.at[k],
            send_sem=term_sem.at[0],
            recv_sem=term_sem.at[1],
            device_id=device(ahead(k)),
            device_id_type=MESH,
        ).start()
        return carry

    lax.fori_loop(1, N, send_term, 0)

    for i in range(2):
        image = pl.ds(M * i, M)
        token_grad[image, :] = (
            dot(dispatch[image, :].astype(BF16), parts[2 + i]) + dot(lows[i], router_rel[...], 1, 1)
        ).astype(BF16)
    stores[2].start()

    pltpu.make_async_copy(terms_in, terms_in, term_sem.at[1]).wait()
    own_sum[...] = jnp.sum(terms_in[...].astype(F32), axis=0).astype(BF16)
    pltpu.make_async_copy(own_sum, block(gathered, me), gather_sem.at[1]).start()

    def send_sum(k, carry):
        pltpu.make_async_remote_copy(
            src_ref=own_sum,
            dst_ref=block(gathered, me),
            send_sem=gather_sem.at[0],
            recv_sem=gather_sem.at[1],
            device_id=device(ahead(k)),
            device_id_type=MESH,
        ).start()
        return carry

    lax.fori_loop(1, N, send_sum, 0)
    pltpu.make_async_copy(gathered, gathered, gather_sem.at[1]).wait()
    router_grad[:, :128] = gathered[0].astype(F32)
    router_grad[:, 128:] = gathered[1].astype(F32)
    stores[3].start()

    most = pl.ds(1, N - 1)
    pltpu.make_async_copy(send_buf.at[most], send_buf.at[most], send_sem).wait()
    pltpu.make_async_copy(back_buf.at[most], back_buf.at[most], back_send_sem).wait()
    pltpu.make_async_copy(terms_in.at[most], terms_in.at[most], term_sem.at[0]).wait()
    pltpu.make_async_copy(terms_in.at[most], terms_in.at[most], gather_sem.at[0]).wait()
    for store in stores:
        store.wait()


def local(tokens, router, expert_in, expert_out, upstream):
    hbm = pl.BlockSpec(memory_space=pl.ANY)
    vmem = pltpu.VMEM
    dma = pltpu.SemaphoreType.DMA
    token_grad, router_grad, first_grad, second_grad = pl.pallas_call(
        kernel,
        out_shape=(
            jax.ShapeDtypeStruct((2 * M, WIDTH), BF16),
            jax.ShapeDtypeStruct((WIDTH, SLOTS), F32),
            jax.ShapeDtypeStruct((1, WIDTH, FF), BF16),
            jax.ShapeDtypeStruct((1, FF, WIDTH), BF16),
        ),
        in_specs=[hbm] * 5,
        out_specs=(hbm,) * 4,
        scratch_shapes=[
            vmem((2 * M, WIDTH), BF16),
            vmem((WIDTH, SLOTS), BF16),
            vmem((WIDTH, FF), BF16),
            vmem((FF, WIDTH), BF16),
            vmem((2 * M, WIDTH), BF16),
            vmem((WIDTH, SLOTS), BF16),
            vmem((SLOTS, SLOTS), BF16),
            vmem((CHUNK, CHUNK), BF16),
            vmem((2 * M, SLOTS), F32),
            vmem((2 * M, SLOTS), F32),
            vmem((4, SLOTS, WIDTH), BF16),
            vmem((N, ROWS, WIDTH), BF16),
            vmem((N, ROWS, WIDTH), BF16),
            vmem((4 * N, WIDTH), BF16),
            vmem((4 * N, WIDTH), BF16),
            vmem((4 * N, FF), BF16),
            vmem((4 * N, FF), BF16),
            vmem((HALF, WIDTH), F32),
            vmem((HALF, WIDTH), F32),
            vmem((N, ROWS, WIDTH), BF16),
            vmem((N, ROWS, WIDTH), BF16),
            vmem((WIDTH, FF), BF16),
            vmem((FF, WIDTH), BF16),
            vmem((2 * M, WIDTH), BF16),
            vmem((2 * M, SLOTS), BF16),
            vmem((2, WIDTH, 128), BF16),
            vmem((N, 16, 128), BF16),
            vmem((16, 128), BF16),
            vmem((2, WIDTH, 128), BF16),
            vmem((WIDTH, SLOTS), F32),
            dma((5,)),
            dma((4,)),
            dma,
            dma((GROUPS,)),
            dma,
            dma,
            dma((2,)),
            dma((2,)),
        ],
        compiler_params=pltpu.CompilerParams(
            collective_id=0, has_side_effects=True, vmem_limit_bytes=56 << 20
        ),
        cost_estimate=pl.CostEstimate(flops=16 * 10**9, bytes_accessed=24 * 10**6, transcendentals=2 * 10**6),
    )(tokens, router, expert_in, expert_out, upstream)
    return (token_grad, router_grad, first_grad, second_grad)


def solution(mesh):
    return jax.shard_map(
        local,
        mesh=mesh,
        in_specs=(
            P(("wide", "narrow"), None),
            P(),
            P(("wide", "narrow"), None, None),
            P(("wide", "narrow"), None, None),
            P(("wide", "narrow"), None),
        ),
        out_specs=(
            P(("wide", "narrow"), None),
            P(),
            P(("wide", "narrow"), None, None),
            P(("wide", "narrow"), None, None),
        ),
        check_vma=False,
    )
```

```python
import math

import jax
import jax.numpy as jnp
from jax import lax
from jax.experimental import pallas as pl
from jax.experimental.pallas import tpu as pltpu
from jax.sharding import PartitionSpec as P

MESH = pl.DeviceIdType.MESH
F32 = jnp.float32
BF16 = jnp.bfloat16
N = 128
WIDTH = 1024
FF = 2048
M = 256
SLOTS = 256
ROWS = 8
GROUP = 32
GROUPS = N // GROUP
CHIPS = N // 2
NEAR = 16
FAR = N // NEAR - 1
CHUNK = GROUP * ROWS
HALF = CHUNK // 2
FTILE = 512
STRIDE = 37

root_two_pi = math.sqrt(2.0 / math.pi)
cubic_coef = 0.044715


def dot(a, b, ca=1, cb=0):
    return lax.dot_general(a, b, (((ca,), (cb,)), ((), ())), preferred_element_type=F32)


def kernel(
    tokens_hbm,
    router_hbm,
    first_hbm,
    second_hbm,
    upstream_hbm,
    token_grad,
    router_grad,
    first_grad,
    second_grad,
    tokens,
    router,
    first,
    second,
    upstream,
    router_rel,
    turn,
    interleave,
    dispatch,
    combine,
    parts,
    send_buf,
    recv_buf,
    rows_in,
    rows_grad,
    active,
    pre_grad,
    out_acc,
    back_acc,
    back_buf,
    return_buf,
    logit_abs,
    terms,
    pair_in,
    chip_sum,
    terms_in,
    own_sum,
    gathered,
    load_sem,
    send_sem,
    recv_sem,
    back_send_sem,
    back_recv_sem,
    term_sem,
    gather_sem,
    pair_sem,
    whole_sem,
    round_sem,
):
    me = lax.axis_index("wide") * 4 + lax.axis_index("narrow")

    def device(number):
        return (number // 4, number % 4)

    def ahead(k):
        return (me + STRIDE * k) % N

    def behind(k):
        return (me + (N - STRIDE) * k) % N

    loads = [
        pltpu.make_async_copy(src, dst, load_sem.at[n])
        for n, (src, dst) in enumerate(
            (
                (router_hbm, router),
                (tokens_hbm, tokens),
                (upstream_hbm, upstream),
                (first_hbm.at[0], first),
                (second_hbm.at[0], second),
            )
        )
    ]
    for load in loads:
        load.start()

    barrier = pltpu.get_barrier_semaphore()

    def greet(k, carry):
        pl.semaphore_signal(barrier, inc=1, device_id=device((me + k) % N), device_id_type=MESH)
        return carry

    lax.fori_loop(1, N, greet, 0)

    row = lax.broadcasted_iota(jnp.int32, (SLOTS, SLOTS), 0)
    col = lax.broadcasted_iota(jnp.int32, (SLOTS, SLOTS), 1)
    slot = 2 * ((me + STRIDE * (col >> 1)) & (N - 1)) + (col & 1)
    turn[...] = jnp.where(row == slot, 1.0, 0.0).astype(BF16)
    row = lax.broadcasted_iota(jnp.int32, (CHUNK, CHUNK), 0)
    col = lax.broadcasted_iota(jnp.int32, (CHUNK, CHUNK), 1)
    origin = ((row >> 1) & 3) * (2 * GROUP) + 2 * (row >> 3) + (row & 1)
    interleave[...] = jnp.where(col == origin, 1.0, 0.0).astype(BF16)

    loads[0].wait()
    router_rel[...] = dot(router[...], turn[...]).astype(BF16)
    loads[1].wait()
    loads[2].wait()
    for i in range(2):
        image = pl.ds(M * i, M)
        logits = dot(tokens[image, :], router_rel[...])
        top = jnp.exp(logits - jnp.max(logits, axis=0, keepdims=True))
        disp = top / jnp.sum(top, axis=0, keepdims=True)
        top = jnp.exp(logits - jnp.max(logits, axis=1, keepdims=True))
        comb = top / jnp.sum(top, axis=1, keepdims=True)
        dispatch[image, :] = disp
        combine[image, :] = comb
        parts[i] = dot(disp.astype(BF16), tokens[image, :], 0, 0).astype(BF16)
        parts[2 + i] = dot(comb.astype(BF16), upstream[image, :], 0, 0).astype(BF16)

    pl.semaphore_wait(barrier, N - 1)
    def send_copy(k):
        return pltpu.make_async_remote_copy(
            src_ref=send_buf.at[k],
            dst_ref=recv_buf.at[k],
            send_sem=send_sem,
            recv_sem=recv_sem.at[k // GROUP],
            device_id=device(ahead(k)),
            device_id_type=MESH,
        )

    own = pltpu.make_async_copy(send_buf.at[0], recv_buf.at[0], recv_sem.at[0])
    for g in range(GROUPS):
        stack = parts[:, 2 * GROUP * g : 2 * GROUP * (g + 1), :].reshape(CHUNK, WIDTH)
        send_buf[GROUP * g : GROUP * (g + 1)] = (
            dot(interleave[...], stack).astype(BF16).reshape(GROUP, ROWS, WIDTH)
        )
        if g == 0:
            own.start()

        def send(k, carry):
            send_copy(k).start()
            return carry

        if g == 0:
            lax.fori_loop(1, NEAR, send, 0)
            lax.fori_loop(NEAR, GROUP, send, 0)
        else:
            lax.fori_loop(GROUP * g, GROUP * (g + 1), send, 0)

    loads[3].wait()
    loads[4].wait()

    def back_copy(k):
        return pltpu.make_async_remote_copy(
            src_ref=back_buf.at[k],
            dst_ref=return_buf.at[k],
            send_sem=back_send_sem,
            recv_sem=back_recv_sem,
            device_id=device(behind(k)),
            device_id_type=MESH,
        )

    def expert(g, carry):
        group = pl.ds(pl.multiple_of(g * GROUP, GROUP), GROUP)
        rows = pl.ds(pl.multiple_of(g * HALF, HALF), HALF)
        pltpu.make_async_copy(recv_buf.at[group], recv_buf.at[group], recv_sem.at[g]).wait()
        split = dot(interleave[...], recv_buf[group].reshape(CHUNK, WIDTH), 0, 0).astype(BF16)
        rows_in[rows, :] = split[:HALF]
        rows_grad[rows, :] = split[HALF:]
        out_acc[...] = jnp.zeros_like(out_acc)
        back_acc[...] = jnp.zeros_like(back_acc)

        def tile(t, inner):
            cols = pl.ds(pl.multiple_of(t * FTILE, FTILE), FTILE)
            hidden = dot(rows_in[rows, :], first[:, cols])
            grad = dot(rows_grad[rows, :], second[cols, :], 1, 1)
            square = hidden * hidden
            tangent = jnp.tanh(root_two_pi * (hidden + cubic_coef * square * hidden))
            act = (0.5 * hidden * (1.0 + tangent)).astype(BF16)
            slope = 0.5 * (1.0 + tangent) + 0.5 * hidden * (1.0 - tangent * tangent) * root_two_pi * (
                1.0 + 3.0 * cubic_coef * square
            )
            pre = (grad * slope).astype(BF16)
            active[rows, cols] = act
            pre_grad[rows, cols] = pre
            out_acc[...] += dot(act, second[cols, :])
            back_acc[...] += dot(pre, first[:, cols], 1, 1)
            return inner

        lax.fori_loop(0, FF // FTILE, tile, 0)
        both = jnp.concatenate([out_acc[...].astype(BF16), back_acc[...].astype(BF16)], axis=0)
        back_buf[group] = dot(interleave[...], both).astype(BF16).reshape(GROUP, ROWS, WIDTH)

        @pl.when(g == 0)
        def _():
            pltpu.make_async_copy(back_buf.at[0], return_buf.at[0], back_recv_sem).start()

        def send(k, inner):
            back_copy(k).start()
            return inner

        lax.fori_loop(jnp.maximum(1, GROUP * g), GROUP * (g + 1), send, 0)
        return carry

    lax.fori_loop(0, GROUPS, expert, 0)

    def weights(t, carry):
        cols = pl.ds(pl.multiple_of(t * FTILE, FTILE), FTILE)
        second_grad[0, cols, :] = dot(active[:, cols], rows_grad[...], 0, 0).astype(BF16)
        first_grad[0, :, cols] = dot(rows_in[...], pre_grad[:, cols], 0, 0).astype(BF16)
        return carry

    lax.fori_loop(0, FF // FTILE, weights, 0)
    pltpu.make_async_copy(return_buf, return_buf, back_recv_sem).wait()
    for g in range(GROUPS):
        chunk = return_buf[GROUP * g : GROUP * (g + 1)].reshape(CHUNK, WIDTH)
        split = dot(interleave[...], chunk, 0, 0).astype(BF16)
        parts[:, 2 * GROUP * g : 2 * GROUP * (g + 1), :] = split.reshape(4, 2 * GROUP, WIDTH)
    lows = []
    for i in range(2):
        image = pl.ds(M * i, M)
        disp = dispatch[image, :]
        comb = combine[image, :]
        combine_grad = dot(upstream[image, :], parts[i], 1, 1)
        dispatch_grad = dot(tokens[image, :], parts[2 + i], 1, 1)
        logit_grad = disp * (dispatch_grad - jnp.sum(disp * dispatch_grad, axis=0, keepdims=True))
        logit_grad = logit_grad + comb * (
            combine_grad - jnp.sum(comb * combine_grad, axis=1, keepdims=True)
        )
        low = logit_grad.astype(BF16)
        lows.append(low)
        logit_abs[image, :] = dot(low, turn[...], 1, 1).astype(BF16)
    total = dot(tokens[...], logit_abs[...], 0, 0).astype(BF16)
    terms[0] = total[:, :128]
    terms[1] = total[:, 128:]

    core = me % 2
    partner = device(me + 1 - 2 * core)

    pair = pltpu.make_async_remote_copy(
        src_ref=terms.at[1 - core],
        dst_ref=pair_in,
        send_sem=pair_sem.at[0],
        recv_sem=pair_sem.at[1],
        device_id=partner,
        device_id_type=MESH,
    )
    pair.start()
    pair.wait_recv()
    chip_sum[...] = (
        (terms[core].astype(F32) + pair_in[...].astype(F32)).astype(BF16).reshape(CHIPS, 16, 128)
    )
    pltpu.make_async_copy(chip_sum.at[me // 2], terms_in.at[0], term_sem.at[1]).start()

    def send_term(j, carry):
        pltpu.make_async_remote_copy(
            src_ref=chip_sum.at[ahead(2 * j) // 2],
            dst_ref=terms_in.at[j],
            send_sem=term_sem.at[0],
            recv_sem=term_sem.at[1],
            device_id=device(ahead(2 * j)),
            device_id_type=MESH,
        ).start()
        return carry

    lax.fori_loop(1, CHIPS, send_term, 0)

    for i in range(2):
        image = pl.ds(M * i, M)
        token_grad[image, :] = (
            dot(dispatch[image, :].astype(BF16), parts[2 + i]) + dot(lows[i], router_rel[...], 1, 1)
        ).astype(BF16)

    pltpu.make_async_copy(terms_in, terms_in, term_sem.at[1]).wait()
    own_sum[...] = jnp.sum(terms_in[...].astype(F32), axis=0).astype(BF16)
    pltpu.make_async_copy(own_sum, gathered.at[core, me // 2], gather_sem.at[1]).start()

    def send_sum(j, carry):
        pltpu.make_async_remote_copy(
            src_ref=own_sum,
            dst_ref=gathered.at[core, me // 2],
            send_sem=gather_sem.at[0],
            recv_sem=gather_sem.at[1],
            device_id=device(ahead(2 * j)),
            device_id_type=MESH,
        ).start()
        return carry

    lax.fori_loop(1, CHIPS, send_sum, 0)
    pltpu.make_async_copy(gathered.at[core], gathered.at[core], gather_sem.at[1]).wait()
    whole = pltpu.make_async_remote_copy(
        src_ref=gathered.at[core],
        dst_ref=gathered.at[core],
        send_sem=whole_sem.at[0],
        recv_sem=whole_sem.at[1],
        device_id=partner,
        device_id_type=MESH,
    )
    whole.start()
    whole.wait()
    pair.wait_send()
    router_grad[:, :128] = gathered[0].reshape(WIDTH, 128).astype(F32)
    router_grad[:, 128:] = gathered[1].reshape(WIDTH, 128).astype(F32)

    most = pl.ds(1, N - 1)
    pltpu.make_async_copy(send_buf.at[most], send_buf.at[most], send_sem).wait()
    pltpu.make_async_copy(back_buf.at[most], back_buf.at[most], back_send_sem).wait()
    most = pl.ds(1, CHIPS - 1)
    pltpu.make_async_copy(terms_in.at[most], terms_in.at[most], term_sem.at[0]).wait()
    pltpu.make_async_copy(terms_in.at[most], terms_in.at[most], gather_sem.at[0]).wait()


def store_kernel(*refs):
    ins, outs, sem = refs[:4], refs[4:8], refs[8]
    copies = [pltpu.make_async_copy(ins[n], outs[n], sem.at[n]) for n in range(4)]
    for copy in copies:
        copy.start()
    for copy in copies:
        copy.wait()


def local(tokens, router, expert_in, expert_out, upstream):
    hbm = pl.BlockSpec(memory_space=pl.ANY)
    vmem = pltpu.VMEM
    dma = pltpu.SemaphoreType.DMA
    shapes = (
        ((2 * M, WIDTH), BF16),
        ((WIDTH, SLOTS), F32),
        ((1, WIDTH, FF), BF16),
        ((1, FF, WIDTH), BF16),
    )
    outs = pl.pallas_call(
        kernel,
        out_shape=tuple(vmem(*shape) for shape in shapes),
        in_specs=[pl.BlockSpec(memory_space=pltpu.HBM)] * 5,
        out_specs=(pl.BlockSpec(memory_space=vmem),) * 4,
        scratch_shapes=[
            vmem((2 * M, WIDTH), BF16),
            vmem((WIDTH, SLOTS), BF16),
            vmem((WIDTH, FF), BF16),
            vmem((FF, WIDTH), BF16),
            vmem((2 * M, WIDTH), BF16),
            vmem((WIDTH, SLOTS), BF16),
            vmem((SLOTS, SLOTS), BF16),
            vmem((CHUNK, CHUNK), BF16),
            vmem((2 * M, SLOTS), F32),
            vmem((2 * M, SLOTS), F32),
            vmem((4, SLOTS, WIDTH), BF16),
            vmem((N, ROWS, WIDTH), BF16),
            vmem((N, ROWS, WIDTH), BF16),
            vmem((4 * N, WIDTH), BF16),
            vmem((4 * N, WIDTH), BF16),
            vmem((4 * N, FF), BF16),
            vmem((4 * N, FF), BF16),
            vmem((HALF, WIDTH), F32),
            vmem((HALF, WIDTH), F32),
            vmem((N, ROWS, WIDTH), BF16),
            vmem((N, ROWS, WIDTH), BF16),
            vmem((2 * M, SLOTS), BF16),
            vmem((2, WIDTH, 128), BF16),
            vmem((WIDTH, 128), BF16),
            vmem((CHIPS, 16, 128), BF16),
            vmem((CHIPS, 16, 128), BF16),
            vmem((16, 128), BF16),
            vmem((2, CHIPS, 16, 128), BF16),
            dma((5,)),
            dma,
            dma((GROUPS,)),
            dma,
            dma,
            dma((2,)),
            dma((2,)),
            dma((2,)),
            dma((2,)),
            pltpu.SemaphoreType.REGULAR,
        ],
        compiler_params=pltpu.CompilerParams(
            collective_id=0, has_side_effects=True, vmem_limit_bytes=50 << 20
        ),
        cost_estimate=pl.CostEstimate(
            flops=16 * 10**9, bytes_accessed=12 * 10**6, transcendentals=2 * 10**6
        ),
    )(tokens, router, expert_in, expert_out, upstream)
    return pl.pallas_call(
        store_kernel,
        out_shape=tuple(jax.ShapeDtypeStruct(*shape) for shape in shapes),
        in_specs=[pl.BlockSpec(memory_space=vmem)] * 4,
        out_specs=(hbm,) * 4,
        scratch_shapes=[dma((4,))],
        compiler_params=pltpu.CompilerParams(vmem_limit_bytes=16 << 20),
        cost_estimate=pl.CostEstimate(flops=0, bytes_accessed=10 * 10**6, transcendentals=0),
    )(*outs)


def solution(mesh):
    return jax.shard_map(
        local,
        mesh=mesh,
        in_specs=(
            P(("wide", "narrow"), None),
            P(),
            P(("wide", "narrow"), None, None),
            P(("wide", "narrow"), None, None),
            P(("wide", "narrow"), None),
        ),
        out_specs=(
            P(("wide", "narrow"), None),
            P(),
            P(("wide", "narrow"), None, None),
            P(("wide", "narrow"), None, None),
        ),
        check_vma=False,
    )
```

```python
import math

import jax
import jax.numpy as jnp
from jax import lax
from jax.experimental import pallas as pl
from jax.experimental.pallas import tpu as pltpu
from jax.sharding import PartitionSpec as P

MESH = pl.DeviceIdType.MESH
F32 = jnp.float32
BF16 = jnp.bfloat16
N = 128
WIDTH = 1024
FF = 2048
M = 256
SLOTS = 256
ROWS = 8
GROUP = 32
GROUPS = N // GROUP
CHIPS = N // 2
NEAR = 16
FAR = N // NEAR - 1
CHUNK = GROUP * ROWS
HALF = CHUNK // 2
FTILE = 512
STRIDE = 37

root_two_pi = math.sqrt(2.0 / math.pi)
cubic_coef = 0.044715


def dot(a, b, ca=1, cb=0):
    return lax.dot_general(a, b, (((ca,), (cb,)), ((), ())), preferred_element_type=F32)


def kernel(
    tokens_hbm,
    router_hbm,
    first_hbm,
    second_hbm,
    upstream_hbm,
    token_grad,
    router_grad,
    first_grad,
    second_grad,
    tokens,
    router,
    first,
    second,
    upstream,
    router_rel,
    turn,
    interleave,
    separate,
    dispatch,
    combine,
    parts,
    send_buf,
    recv_buf,
    rows_in,
    rows_grad,
    active,
    pre_grad,
    out_acc,
    back_acc,
    back_buf,
    return_buf,
    upright,
    router_flat,
    flipped,
    grads,
    logit_abs,
    terms,
    pair_in,
    chip_sum,
    terms_in,
    own_sum,
    gathered,
    load_sem,
    send_sem,
    recv_sem,
    back_send_sem,
    back_recv_sem,
    term_sem,
    gather_sem,
    pair_sem,
    whole_sem,
    round_sem,
):
    me = lax.axis_index("wide") * 4 + lax.axis_index("narrow")

    def device(number):
        return (number // 4, number % 4)

    def ahead(k):
        return (me + STRIDE * k) % N

    def behind(k):
        return (me + (N - STRIDE) * k) % N

    loads = [
        pltpu.make_async_copy(src, dst, load_sem.at[n])
        for n, (src, dst) in enumerate(
            (
                (router_hbm, router),
                (tokens_hbm, tokens),
                (upstream_hbm, upstream),
                (first_hbm.at[0], first),
                (second_hbm.at[0], second),
            )
        )
    ]

    barrier = pltpu.get_barrier_semaphore()

    def greet(k, carry):
        pl.semaphore_signal(barrier, inc=1, device_id=device(behind(k)), device_id_type=MESH)
        return carry

    def greet_far(k, carry):
        return greet(NEAR * k, carry)

    lax.fori_loop(1, NEAR, greet, 0)
    lax.fori_loop(1, FAR + 1, greet_far, 0)
    for load in loads[:3]:
        load.start()

    row = lax.broadcasted_iota(jnp.int32, (SLOTS, SLOTS), 0)
    col = lax.broadcasted_iota(jnp.int32, (SLOTS, SLOTS), 1)
    slot = 2 * ((me + STRIDE * (col >> 1)) & (N - 1)) + (col & 1)
    turn[...] = jnp.where(row == slot, 1.0, 0.0).astype(BF16)
    row = lax.broadcasted_iota(jnp.int32, (CHUNK, CHUNK), 0)
    col = lax.broadcasted_iota(jnp.int32, (CHUNK, CHUNK), 1)
    origin = ((row >> 1) & 3) * (2 * GROUP) + 2 * (row >> 3) + (row & 1)
    interleave[...] = jnp.where(col == origin, 1.0, 0.0).astype(BF16)
    origin = ((col >> 1) & 3) * (2 * GROUP) + 2 * (col >> 3) + (col & 1)
    separate[...] = jnp.where(row == origin, 1.0, 0.0).astype(BF16)

    loads[0].wait()
    router_rel[...] = dot(router[...], turn[...]).astype(BF16)
    pl.semaphore_wait(barrier, NEAR - 1 + FAR)

    def tell(k, carry):
        pl.semaphore_signal(
            round_sem, inc=1, device_id=device(behind(NEAR * k)), device_id_type=MESH
        )
        return carry

    lax.fori_loop(1, FAR + 1, tell, 0)
    loads[1].wait()
    loads[2].wait()
    loads[3].start()
    loads[4].start()
    lows = []
    for i in range(2):
        image = pl.ds(M * i, M)
        logits = dot(tokens[image, :], router_rel[...])
        top = jnp.exp(logits - jnp.max(logits, axis=0, keepdims=True))
        disp = top / jnp.sum(top, axis=0, keepdims=True)
        top = jnp.exp(logits - jnp.max(logits, axis=1, keepdims=True))
        comb = top / jnp.sum(top, axis=1, keepdims=True)
        dispatch[image, :] = disp
        combine[image, :] = comb
        lows.append((disp.astype(BF16), comb.astype(BF16)))

    def send_copy(k):
        return pltpu.make_async_remote_copy(
            src_ref=send_buf.at[k],
            dst_ref=recv_buf.at[k],
            send_sem=send_sem,
            recv_sem=recv_sem.at[k // GROUP],
            device_id=device(ahead(k)),
            device_id_type=MESH,
        )

    own = pltpu.make_async_copy(send_buf.at[0], recv_buf.at[0], recv_sem.at[0])
    for g in range(GROUPS):
        if g % 2 == 0:
            slots = slice(2 * GROUP * g, 2 * GROUP * (g + 2))
            for i in range(2):
                image = pl.ds(M * i, M)
                parts[i, slots, :] = dot(lows[i][0][:, slots], tokens[image, :], 0, 0).astype(BF16)
                parts[2 + i, slots, :] = dot(lows[i][1][:, slots], upstream[image, :], 0, 0).astype(
                    BF16
                )
        stack = parts[:, 2 * GROUP * g : 2 * GROUP * (g + 1), :].reshape(CHUNK, WIDTH)
        send_buf[GROUP * g : GROUP * (g + 1)] = (
            dot(interleave[...], stack).astype(BF16).reshape(GROUP, ROWS, WIDTH)
        )
        if g == 0:
            own.start()
            pl.semaphore_wait(round_sem, FAR)

        def send(k, carry):
            send_copy(k).start()
            return carry

        if g == 0:
            lax.fori_loop(1, NEAR, send, 0)
            lax.fori_loop(NEAR, GROUP, send, 0)
        else:
            lax.fori_loop(GROUP * g, GROUP * (g + 1), send, 0)

    loads[3].wait()
    loads[4].wait()

    def back_copy(k):
        return pltpu.make_async_remote_copy(
            src_ref=back_buf.at[k],
            dst_ref=return_buf.at[k],
            send_sem=back_send_sem,
            recv_sem=back_recv_sem.at[k // GROUP],
            device_id=device(behind(k)),
            device_id_type=MESH,
        )

    def expert(g, carry):
        group = pl.ds(pl.multiple_of(g * GROUP, GROUP), GROUP)
        rows = pl.ds(pl.multiple_of(g * HALF, HALF), HALF)
        pltpu.make_async_copy(recv_buf.at[group], recv_buf.at[group], recv_sem.at[g]).wait()
        split = dot(separate[...], recv_buf[group].reshape(CHUNK, WIDTH)).astype(BF16)
        rows_in[rows, :] = split[:HALF]
        rows_grad[rows, :] = split[HALF:]
        out_acc[...] = jnp.zeros_like(out_acc)
        back_acc[...] = jnp.zeros_like(back_acc)

        def tile(t, inner):
            cols = pl.ds(pl.multiple_of(t * FTILE, FTILE), FTILE)
            hidden = dot(rows_in[rows, :], first[:, cols])
            grad = dot(rows_grad[rows, :], second[cols, :], 1, 1)
            square = hidden * hidden
            tangent = jnp.tanh(root_two_pi * (hidden + cubic_coef * square * hidden))
            act = (0.5 * hidden * (1.0 + tangent)).astype(BF16)
            slope = 0.5 * (1.0 + tangent) + 0.5 * hidden * (1.0 - tangent * tangent) * root_two_pi * (
                1.0 + 3.0 * cubic_coef * square
            )
            pre = (grad * slope).astype(BF16)
            active[rows, cols] = act
            pre_grad[rows, cols] = pre
            out_acc[...] += dot(act, second[cols, :])
            back_acc[...] += dot(pre, first[:, cols], 1, 1)
            return inner

        lax.fori_loop(0, FF // FTILE, tile, 0)
        both = jnp.concatenate([out_acc[...].astype(BF16), back_acc[...].astype(BF16)], axis=0)
        back_buf[group] = dot(interleave[...], both).astype(BF16).reshape(GROUP, ROWS, WIDTH)

        @pl.when(g == 0)
        def _():
            pltpu.make_async_copy(back_buf.at[0], return_buf.at[0], back_recv_sem.at[0]).start()

        def send(k, inner):
            back_copy(k).start()
            return inner

        lax.fori_loop(jnp.maximum(1, GROUP * g), GROUP * (g + 1), send, 0)
        return carry

    lax.fori_loop(0, GROUPS, expert, 0)

    def weights(t, carry):
        cols = pl.ds(pl.multiple_of(t * FTILE, FTILE), FTILE)
        second_grad[0, cols, :] = dot(active[:, cols], rows_grad[...], 0, 0).astype(BF16)
        first_grad[0, :, cols] = dot(rows_in[...], pre_grad[:, cols], 0, 0).astype(BF16)
        return carry

    lax.fori_loop(0, FF // FTILE, weights, 0)
    upright[0] = tokens[...].T
    upright[1] = upstream[...].T
    router_flat[...] = router_rel[...].T
    for i in range(2):
        image = pl.ds(M * i, M)
        flipped[0, :, image] = dispatch[image, :].T
        flipped[1, :, image] = combine[image, :].T
    for g in range(GROUPS):
        group = pl.ds(GROUP * g, GROUP)
        pltpu.make_async_copy(
            return_buf.at[group], return_buf.at[group], back_recv_sem.at[g]
        ).wait()
        split = dot(separate[...], return_buf[group].reshape(CHUNK, WIDTH)).astype(BF16)
        parts[:, 2 * GROUP * g : 2 * GROUP * (g + 1), :] = split.reshape(4, 2 * GROUP, WIDTH)
        if g % 2 == 1:
            slots = pl.ds(2 * GROUP * (g - 1), 4 * GROUP)
            for i in range(2):
                image = pl.ds(M * i, M)
                grads[0, slots, image] = dot(parts[i, slots, :], upright[1, :, image])
                grads[1, slots, image] = dot(parts[2 + i, slots, :], upright[0, :, image])
    lows = []
    for i in range(2):
        image = pl.ds(M * i, M)
        disp = flipped[0, :, image]
        comb = flipped[1, :, image]
        combine_grad = grads[0, :, image]
        dispatch_grad = grads[1, :, image]
        logit_grad = disp * (dispatch_grad - jnp.sum(disp * dispatch_grad, axis=1, keepdims=True))
        logit_grad = logit_grad + comb * (
            combine_grad - jnp.sum(comb * combine_grad, axis=0, keepdims=True)
        )
        low = logit_grad.astype(BF16)
        lows.append(low)
        logit_abs[:, image] = dot(turn[...], low).astype(BF16)

    core = me % 2
    partner = device(me + 1 - 2 * core)

    pair = pltpu.make_async_remote_copy(
        src_ref=terms,
        dst_ref=pair_in,
        send_sem=pair_sem.at[0],
        recv_sem=pair_sem.at[1],
        device_id=partner,
        device_id_type=MESH,
    )

    def half(which):
        return logit_abs[pl.ds(pl.multiple_of(which * 128, 128), 128), :]

    terms[...] = dot(upright[0], half(1 - core), 1, 1).astype(BF16)
    pair.start()
    own_terms = dot(upright[0], half(core), 1, 1)
    pair.wait_recv()
    chip_sum[...] = (
        (own_terms + pair_in[...].astype(F32)).astype(BF16).reshape(CHIPS, 16, 128)
    )
    pltpu.make_async_copy(chip_sum.at[me // 2], terms_in.at[0], term_sem.at[1]).start()

    def send_term(j, carry):
        pltpu.make_async_remote_copy(
            src_ref=chip_sum.at[ahead(2 * j) // 2],
            dst_ref=terms_in.at[j],
            send_sem=term_sem.at[0],
            recv_sem=term_sem.at[1],
            device_id=device(ahead(2 * j)),
            device_id_type=MESH,
        ).start()
        return carry

    lax.fori_loop(1, CHIPS, send_term, 0)

    for i in range(2):
        image = pl.ds(M * i, M)
        token_grad[image, :] = (
            dot(dispatch[image, :].astype(BF16), parts[2 + i]) + dot(lows[i], router_flat[...], 0, 0)
        ).astype(BF16)

    pltpu.make_async_copy(terms_in, terms_in, term_sem.at[1]).wait()
    own_sum[...] = jnp.sum(terms_in[...].astype(F32), axis=0).astype(BF16)
    pltpu.make_async_copy(own_sum, gathered.at[core, me // 2], gather_sem.at[1]).start()

    def send_sum(j, carry):
        pltpu.make_async_remote_copy(
            src_ref=own_sum,
            dst_ref=gathered.at[core, me // 2],
            send_sem=gather_sem.at[0],
            recv_sem=gather_sem.at[1],
            device_id=device(ahead(2 * j)),
            device_id_type=MESH,
        ).start()
        return carry

    lax.fori_loop(1, CHIPS, send_sum, 0)
    pltpu.make_async_copy(gathered.at[core], gathered.at[core], gather_sem.at[1]).wait()
    whole = pltpu.make_async_remote_copy(
        src_ref=gathered.at[core],
        dst_ref=gathered.at[core],
        send_sem=whole_sem.at[0],
        recv_sem=whole_sem.at[1],
        device_id=partner,
        device_id_type=MESH,
    )
    whole.start()
    whole.wait()
    pair.wait_send()
    router_grad[:, :128] = gathered[0].reshape(WIDTH, 128).astype(F32)
    router_grad[:, 128:] = gathered[1].reshape(WIDTH, 128).astype(F32)

    most = pl.ds(1, N - 1)
    pltpu.make_async_copy(send_buf.at[most], send_buf.at[most], send_sem).wait()
    pltpu.make_async_copy(back_buf.at[most], back_buf.at[most], back_send_sem).wait()
    most = pl.ds(1, CHIPS - 1)
    pltpu.make_async_copy(terms_in.at[most], terms_in.at[most], term_sem.at[0]).wait()
    pltpu.make_async_copy(terms_in.at[most], terms_in.at[most], gather_sem.at[0]).wait()


def store_kernel(*refs):
    ins, outs, sem = refs[:4], refs[4:8], refs[8]
    copies = [pltpu.make_async_copy(ins[n], outs[n], sem.at[n]) for n in range(4)]
    for copy in copies:
        copy.start()
    for copy in copies:
        copy.wait()


def local(tokens, router, expert_in, expert_out, upstream):
    hbm = pl.BlockSpec(memory_space=pl.ANY)
    vmem = pltpu.VMEM
    dma = pltpu.SemaphoreType.DMA
    shapes = (
        ((2 * M, WIDTH), BF16),
        ((WIDTH, SLOTS), F32),
        ((1, WIDTH, FF), BF16),
        ((1, FF, WIDTH), BF16),
    )
    outs = pl.pallas_call(
        kernel,
        out_shape=tuple(vmem(*shape) for shape in shapes),
        in_specs=[pl.BlockSpec(memory_space=pltpu.HBM)] * 5,
        out_specs=(pl.BlockSpec(memory_space=vmem),) * 4,
        scratch_shapes=[
            vmem((2 * M, WIDTH), BF16),
            vmem((WIDTH, SLOTS), BF16),
            vmem((WIDTH, FF), BF16),
            vmem((FF, WIDTH), BF16),
            vmem((2 * M, WIDTH), BF16),
            vmem((WIDTH, SLOTS), BF16),
            vmem((SLOTS, SLOTS), BF16),
            vmem((CHUNK, CHUNK), BF16),
            vmem((CHUNK, CHUNK), BF16),
            vmem((2 * M, SLOTS), F32),
            vmem((2 * M, SLOTS), F32),
            vmem((4, SLOTS, WIDTH), BF16),
            vmem((N, ROWS, WIDTH), BF16),
            vmem((N, ROWS, WIDTH), BF16),
            vmem((4 * N, WIDTH), BF16),
            vmem((4 * N, WIDTH), BF16),
            vmem((4 * N, FF), BF16),
            vmem((4 * N, FF), BF16),
            vmem((HALF, WIDTH), F32),
            vmem((HALF, WIDTH), F32),
            vmem((N, ROWS, WIDTH), BF16),
            vmem((N, ROWS, WIDTH), BF16),
            vmem((2, WIDTH, 2 * M), BF16),
            vmem((SLOTS, WIDTH), BF16),
            vmem((2, SLOTS, 2 * M), F32),
            vmem((2, SLOTS, 2 * M), F32),
            vmem((SLOTS, 2 * M), BF16),
            vmem((WIDTH, 128), BF16),
            vmem((WIDTH, 128), BF16),
            vmem((CHIPS, 16, 128), BF16),
            vmem((CHIPS, 16, 128), BF16),
            vmem((16, 128), BF16),
            vmem((2, CHIPS, 16, 128), BF16),
            dma((5,)),
            dma,
            dma((GROUPS,)),
            dma,
            dma((GROUPS,)),
            dma((2,)),
            dma((2,)),
            dma((2,)),
            dma((2,)),
            pltpu.SemaphoreType.REGULAR,
        ],
        compiler_params=pltpu.CompilerParams(
            collective_id=0, has_side_effects=True, vmem_limit_bytes=50 << 20
        ),
        cost_estimate=pl.CostEstimate(
            flops=16 * 10**9, bytes_accessed=12 * 10**6, transcendentals=2 * 10**6
        ),
    )(tokens, router, expert_in, expert_out, upstream)
    return pl.pallas_call(
        store_kernel,
        out_shape=tuple(jax.ShapeDtypeStruct(*shape) for shape in shapes),
        in_specs=[pl.BlockSpec(memory_space=vmem)] * 4,
        out_specs=(hbm,) * 4,
        scratch_shapes=[dma((4,))],
        compiler_params=pltpu.CompilerParams(vmem_limit_bytes=16 << 20),
        cost_estimate=pl.CostEstimate(flops=0, bytes_accessed=10 * 10**6, transcendentals=0),
    )(*outs)


def solution(mesh):
    return jax.shard_map(
        local,
        mesh=mesh,
        in_specs=(
            P(("wide", "narrow"), None),
            P(),
            P(("wide", "narrow"), None, None),
            P(("wide", "narrow"), None, None),
            P(("wide", "narrow"), None),
        ),
        out_specs=(
            P(("wide", "narrow"), None),
            P(),
            P(("wide", "narrow"), None, None),
            P(("wide", "narrow"), None, None),
        ),
        check_vma=False,
    )
```

```python
import math

import jax
import jax.numpy as jnp
from jax import lax
from jax.experimental import pallas as pl
from jax.experimental.pallas import tpu as pltpu
from jax.sharding import PartitionSpec as P

MESH = pl.DeviceIdType.MESH
F32 = jnp.float32
BF16 = jnp.bfloat16
N = 128
WIDTH = 1024
FF = 2048
M = 256
SLOTS = 256
ROWS = 8
GROUP = 32
GROUPS = N // GROUP
CHIPS = N // 2
NEAR = 16
FAR = N // NEAR - 1
CHUNK = GROUP * ROWS
HALF = CHUNK // 2
FTILE = 512
STRIDE = 5

root_two_pi = math.sqrt(2.0 / math.pi)
cubic_coef = 0.044715


def dot(a, b, ca=1, cb=0):
    return lax.dot_general(a, b, (((ca,), (cb,)), ((), ())), preferred_element_type=F32)


def kernel(
    tokens_hbm,
    router_hbm,
    first_hbm,
    second_hbm,
    upstream_hbm,
    token_grad,
    router_grad,
    first_grad,
    second_grad,
    tokens,
    router,
    first,
    second,
    upstream,
    router_rel,
    turn,
    interleave,
    separate,
    dispatch,
    combine,
    parts,
    send_buf,
    recv_buf,
    rows_in,
    rows_grad,
    active,
    pre_grad,
    out_acc,
    back_acc,
    back_buf,
    return_buf,
    upright,
    router_flat,
    flipped,
    grads,
    logit_abs,
    terms,
    pair_in,
    chip_sum,
    terms_in,
    own_sum,
    gathered,
    load_sem,
    send_sem,
    recv_sem,
    back_send_sem,
    back_recv_sem,
    term_sem,
    gather_sem,
    pair_sem,
    whole_sem,
    round_sem,
):
    me = lax.axis_index("wide") * 4 + lax.axis_index("narrow")

    def device(number):
        return (number // 4, number % 4)

    def ahead(k):
        return (me + STRIDE * k) % N

    def behind(k):
        return (me + (N - STRIDE) * k) % N

    loads = [
        pltpu.make_async_copy(src, dst, load_sem.at[n])
        for n, (src, dst) in enumerate(
            (
                (router_hbm, router),
                (tokens_hbm, tokens),
                (upstream_hbm, upstream),
                (first_hbm.at[0], first),
                (second_hbm.at[0], second),
            )
        )
    ]

    barrier = pltpu.get_barrier_semaphore()

    def greet(k, carry):
        pl.semaphore_signal(barrier, inc=1, device_id=device(behind(k)), device_id_type=MESH)
        return carry

    def greet_far(k, carry):
        return greet(NEAR * k, carry)

    lax.fori_loop(1, NEAR, greet, 0)
    lax.fori_loop(1, FAR + 1, greet_far, 0)
    for load in loads[:3]:
        load.start()

    row = lax.broadcasted_iota(jnp.int32, (SLOTS, SLOTS), 0)
    col = lax.broadcasted_iota(jnp.int32, (SLOTS, SLOTS), 1)
    slot = 2 * ((me + STRIDE * (col >> 1)) & (N - 1)) + (col & 1)
    turn[...] = jnp.where(row == slot, 1.0, 0.0).astype(BF16)
    row = lax.broadcasted_iota(jnp.int32, (CHUNK, CHUNK), 0)
    col = lax.broadcasted_iota(jnp.int32, (CHUNK, CHUNK), 1)
    origin = ((row >> 1) & 3) * (2 * GROUP) + 2 * (row >> 3) + (row & 1)
    interleave[...] = jnp.where(col == origin, 1.0, 0.0).astype(BF16)
    origin = ((col >> 1) & 3) * (2 * GROUP) + 2 * (col >> 3) + (col & 1)
    separate[...] = jnp.where(row == origin, 1.0, 0.0).astype(BF16)

    loads[0].wait()
    router_rel[...] = dot(router[...], turn[...]).astype(BF16)
    pl.semaphore_wait(barrier, NEAR - 1 + FAR)

    def tell(k, carry):
        pl.semaphore_signal(
            round_sem, inc=1, device_id=device(behind(NEAR * k)), device_id_type=MESH
        )
        return carry

    lax.fori_loop(1, FAR + 1, tell, 0)
    loads[1].wait()
    loads[2].wait()
    loads[3].start()
    loads[4].start()
    lows = []
    for i in range(2):
        image = pl.ds(M * i, M)
        logits = dot(tokens[image, :], router_rel[...])
        top = jnp.exp(logits - jnp.max(logits, axis=0, keepdims=True))
        disp = top / jnp.sum(top, axis=0, keepdims=True)
        top = jnp.exp(logits - jnp.max(logits, axis=1, keepdims=True))
        comb = top / jnp.sum(top, axis=1, keepdims=True)
        dispatch[image, :] = disp
        combine[image, :] = comb
        lows.append((disp.astype(BF16), comb.astype(BF16)))

    def send_copy(k):
        return pltpu.make_async_remote_copy(
            src_ref=send_buf.at[k],
            dst_ref=recv_buf.at[k],
            send_sem=send_sem,
            recv_sem=recv_sem.at[k // GROUP],
            device_id=device(ahead(k)),
            device_id_type=MESH,
        )

    own = pltpu.make_async_copy(send_buf.at[0], recv_buf.at[0], recv_sem.at[0])
    for g in range(GROUPS):
        if g % 2 == 0:
            slots = slice(2 * GROUP * g, 2 * GROUP * (g + 2))
            for i in range(2):
                image = pl.ds(M * i, M)
                parts[i, slots, :] = dot(lows[i][0][:, slots], tokens[image, :], 0, 0).astype(BF16)
                parts[2 + i, slots, :] = dot(lows[i][1][:, slots], upstream[image, :], 0, 0).astype(
                    BF16
                )
        stack = parts[:, 2 * GROUP * g : 2 * GROUP * (g + 1), :].reshape(CHUNK, WIDTH)
        send_buf[GROUP * g : GROUP * (g + 1)] = (
            dot(interleave[...], stack).astype(BF16).reshape(GROUP, ROWS, WIDTH)
        )
        if g == 0:
            own.start()
            pl.semaphore_wait(round_sem, FAR)

        def send(k, carry):
            send_copy(k).start()
            return carry

        if g == 0:
            lax.fori_loop(1, NEAR, send, 0)
            lax.fori_loop(NEAR, GROUP, send, 0)
        else:
            lax.fori_loop(GROUP * g, GROUP * (g + 1), send, 0)

    loads[3].wait()
    loads[4].wait()

    def back_copy(k):
        return pltpu.make_async_remote_copy(
            src_ref=back_buf.at[k],
            dst_ref=return_buf.at[k],
            send_sem=back_send_sem,
            recv_sem=back_recv_sem.at[k // GROUP],
            device_id=device(behind(k)),
            device_id_type=MESH,
        )

    def expert(g, carry):
        group = pl.ds(pl.multiple_of(g * GROUP, GROUP), GROUP)
        rows = pl.ds(pl.multiple_of(g * HALF, HALF), HALF)
        pltpu.make_async_copy(recv_buf.at[group], recv_buf.at[group], recv_sem.at[g]).wait()
        split = dot(separate[...], recv_buf[group].reshape(CHUNK, WIDTH)).astype(BF16)
        rows_in[rows, :] = split[:HALF]
        rows_grad[rows, :] = split[HALF:]
        out_acc[...] = jnp.zeros_like(out_acc)
        back_acc[...] = jnp.zeros_like(back_acc)

        def tile(t, inner):
            cols = pl.ds(pl.multiple_of(t * FTILE, FTILE), FTILE)
            hidden = dot(rows_in[rows, :], first[:, cols])
            grad = dot(rows_grad[rows, :], second[cols, :], 1, 1)
            square = hidden * hidden
            tangent = jnp.tanh(root_two_pi * (hidden + cubic_coef * square * hidden))
            act = (0.5 * hidden * (1.0 + tangent)).astype(BF16)
            slope = 0.5 * (1.0 + tangent) + 0.5 * hidden * (1.0 - tangent * tangent) * root_two_pi * (
                1.0 + 3.0 * cubic_coef * square
            )
            pre = (grad * slope).astype(BF16)
            active[rows, cols] = act
            pre_grad[rows, cols] = pre
            out_acc[...] += dot(act, second[cols, :])
            back_acc[...] += dot(pre, first[:, cols], 1, 1)
            return inner

        lax.fori_loop(0, FF // FTILE, tile, 0)
        both = jnp.concatenate([out_acc[...].astype(BF16), back_acc[...].astype(BF16)], axis=0)
        back_buf[group] = dot(interleave[...], both).astype(BF16).reshape(GROUP, ROWS, WIDTH)

        @pl.when(g == 0)
        def _():
            pltpu.make_async_copy(back_buf.at[0], return_buf.at[0], back_recv_sem.at[0]).start()

        def send(k, inner):
            back_copy(k).start()
            return inner

        lax.fori_loop(jnp.maximum(1, GROUP * g), GROUP * (g + 1), send, 0)
        return carry

    lax.fori_loop(0, GROUPS, expert, 0)

    def weights(t, carry):
        cols = pl.ds(pl.multiple_of(t * FTILE, FTILE), FTILE)
        second_grad[0, cols, :] = dot(active[:, cols], rows_grad[...], 0, 0).astype(BF16)
        first_grad[0, :, cols] = dot(rows_in[...], pre_grad[:, cols], 0, 0).astype(BF16)
        return carry

    lax.fori_loop(0, FF // FTILE, weights, 0)
    upright[0] = tokens[...].T
    upright[1] = upstream[...].T
    router_flat[...] = router_rel[...].T
    for i in range(2):
        image = pl.ds(M * i, M)
        flipped[0, :, image] = dispatch[image, :].T
        flipped[1, :, image] = combine[image, :].T
    for g in range(GROUPS):
        group = pl.ds(GROUP * g, GROUP)
        pltpu.make_async_copy(
            return_buf.at[group], return_buf.at[group], back_recv_sem.at[g]
        ).wait()
        split = dot(separate[...], return_buf[group].reshape(CHUNK, WIDTH)).astype(BF16)
        parts[:, 2 * GROUP * g : 2 * GROUP * (g + 1), :] = split.reshape(4, 2 * GROUP, WIDTH)
        if g % 2 == 1:
            slots = pl.ds(2 * GROUP * (g - 1), 4 * GROUP)
            for i in range(2):
                image = pl.ds(M * i, M)
                grads[0, slots, image] = dot(parts[i, slots, :], upright[1, :, image])
                grads[1, slots, image] = dot(parts[2 + i, slots, :], upright[0, :, image])
    lows = []
    for i in range(2):
        image = pl.ds(M * i, M)
        disp = flipped[0, :, image]
        comb = flipped[1, :, image]
        combine_grad = grads[0, :, image]
        dispatch_grad = grads[1, :, image]
        logit_grad = disp * (dispatch_grad - jnp.sum(disp * dispatch_grad, axis=1, keepdims=True))
        logit_grad = logit_grad + comb * (
            combine_grad - jnp.sum(comb * combine_grad, axis=0, keepdims=True)
        )
        low = logit_grad.astype(BF16)
        lows.append(low)
        logit_abs[:, image] = dot(turn[...], low).astype(BF16)

    core = me % 2
    partner = device(me + 1 - 2 * core)

    pair = pltpu.make_async_remote_copy(
        src_ref=terms,
        dst_ref=pair_in,
        send_sem=pair_sem.at[0],
        recv_sem=pair_sem.at[1],
        device_id=partner,
        device_id_type=MESH,
    )

    def half(which):
        return logit_abs[pl.ds(pl.multiple_of(which * 128, 128), 128), :]

    terms[...] = dot(upright[0], half(1 - core), 1, 1).astype(BF16)
    pair.start()
    own_terms = dot(upright[0], half(core), 1, 1)
    pair.wait_recv()
    chip_sum[...] = (
        (own_terms + pair_in[...].astype(F32)).astype(BF16).reshape(CHIPS, 16, 128)
    )
    pltpu.make_async_copy(chip_sum.at[me // 2], terms_in.at[0], term_sem.at[1]).start()

    def send_term(j, carry):
        pltpu.make_async_remote_copy(
            src_ref=chip_sum.at[ahead(2 * j) // 2],
            dst_ref=terms_in.at[j],
            send_sem=term_sem.at[0],
            recv_sem=term_sem.at[1],
            device_id=device(ahead(2 * j)),
            device_id_type=MESH,
        ).start()
        return carry

    lax.fori_loop(1, CHIPS, send_term, 0)

    for i in range(2):
        image = pl.ds(M * i, M)
        token_grad[image, :] = (
            dot(dispatch[image, :].astype(BF16), parts[2 + i]) + dot(lows[i], router_flat[...], 0, 0)
        ).astype(BF16)

    pltpu.make_async_copy(terms_in, terms_in, term_sem.at[1]).wait()
    own_sum[...] = jnp.sum(terms_in[...].astype(F32), axis=0).astype(BF16)
    pltpu.make_async_copy(own_sum, gathered.at[core, me // 2], gather_sem.at[1]).start()

    def send_sum(j, carry):
        pltpu.make_async_remote_copy(
            src_ref=own_sum,
            dst_ref=gathered.at[core, me // 2],
            send_sem=gather_sem.at[0],
            recv_sem=gather_sem.at[1],
            device_id=device(ahead(2 * j)),
            device_id_type=MESH,
        ).start()
        return carry

    lax.fori_loop(1, CHIPS, send_sum, 0)
    pltpu.make_async_copy(gathered.at[core], gathered.at[core], gather_sem.at[1]).wait()
    whole = pltpu.make_async_remote_copy(
        src_ref=gathered.at[core],
        dst_ref=gathered.at[core],
        send_sem=whole_sem.at[0],
        recv_sem=whole_sem.at[1],
        device_id=partner,
        device_id_type=MESH,
    )
    whole.start()
    whole.wait()
    pair.wait_send()
    router_grad[:, :128] = gathered[0].reshape(WIDTH, 128).astype(F32)
    router_grad[:, 128:] = gathered[1].reshape(WIDTH, 128).astype(F32)

    most = pl.ds(1, N - 1)
    pltpu.make_async_copy(send_buf.at[most], send_buf.at[most], send_sem).wait()
    pltpu.make_async_copy(back_buf.at[most], back_buf.at[most], back_send_sem).wait()
    most = pl.ds(1, CHIPS - 1)
    pltpu.make_async_copy(terms_in.at[most], terms_in.at[most], term_sem.at[0]).wait()
    pltpu.make_async_copy(terms_in.at[most], terms_in.at[most], gather_sem.at[0]).wait()


def store_kernel(*refs):
    ins, outs, sem = refs[:4], refs[4:8], refs[8]
    copies = [pltpu.make_async_copy(ins[n], outs[n], sem.at[n]) for n in range(4)]
    for copy in copies:
        copy.start()
    for copy in copies:
        copy.wait()


def local(tokens, router, expert_in, expert_out, upstream):
    hbm = pl.BlockSpec(memory_space=pl.ANY)
    vmem = pltpu.VMEM
    dma = pltpu.SemaphoreType.DMA
    shapes = (
        ((2 * M, WIDTH), BF16),
        ((WIDTH, SLOTS), F32),
        ((1, WIDTH, FF), BF16),
        ((1, FF, WIDTH), BF16),
    )
    outs = pl.pallas_call(
        kernel,
        out_shape=tuple(vmem(*shape) for shape in shapes),
        in_specs=[pl.BlockSpec(memory_space=pltpu.HBM)] * 5,
        out_specs=(pl.BlockSpec(memory_space=vmem),) * 4,
        scratch_shapes=[
            vmem((2 * M, WIDTH), BF16),
            vmem((WIDTH, SLOTS), BF16),
            vmem((WIDTH, FF), BF16),
            vmem((FF, WIDTH), BF16),
            vmem((2 * M, WIDTH), BF16),
            vmem((WIDTH, SLOTS), BF16),
            vmem((SLOTS, SLOTS), BF16),
            vmem((CHUNK, CHUNK), BF16),
            vmem((CHUNK, CHUNK), BF16),
            vmem((2 * M, SLOTS), F32),
            vmem((2 * M, SLOTS), F32),
            vmem((4, SLOTS, WIDTH), BF16),
            vmem((N, ROWS, WIDTH), BF16),
            vmem((N, ROWS, WIDTH), BF16),
            vmem((4 * N, WIDTH), BF16),
            vmem((4 * N, WIDTH), BF16),
            vmem((4 * N, FF), BF16),
            vmem((4 * N, FF), BF16),
            vmem((HALF, WIDTH), F32),
            vmem((HALF, WIDTH), F32),
            vmem((N, ROWS, WIDTH), BF16),
            vmem((N, ROWS, WIDTH), BF16),
            vmem((2, WIDTH, 2 * M), BF16),
            vmem((SLOTS, WIDTH), BF16),
            vmem((2, SLOTS, 2 * M), F32),
            vmem((2, SLOTS, 2 * M), F32),
            vmem((SLOTS, 2 * M), BF16),
            vmem((WIDTH, 128), BF16),
            vmem((WIDTH, 128), BF16),
            vmem((CHIPS, 16, 128), BF16),
            vmem((CHIPS, 16, 128), BF16),
            vmem((16, 128), BF16),
            vmem((2, CHIPS, 16, 128), BF16),
            dma((5,)),
            dma,
            dma((GROUPS,)),
            dma,
            dma((GROUPS,)),
            dma((2,)),
            dma((2,)),
            dma((2,)),
            dma((2,)),
            pltpu.SemaphoreType.REGULAR,
        ],
        compiler_params=pltpu.CompilerParams(
            collective_id=0, has_side_effects=True, vmem_limit_bytes=50 << 20
        ),
        cost_estimate=pl.CostEstimate(
            flops=16 * 10**9, bytes_accessed=12 * 10**6, transcendentals=2 * 10**6
        ),
    )(tokens, router, expert_in, expert_out, upstream)
    return pl.pallas_call(
        store_kernel,
        out_shape=tuple(jax.ShapeDtypeStruct(*shape) for shape in shapes),
        in_specs=[pl.BlockSpec(memory_space=vmem)] * 4,
        out_specs=(hbm,) * 4,
        scratch_shapes=[dma((4,))],
        compiler_params=pltpu.CompilerParams(vmem_limit_bytes=16 << 20),
        cost_estimate=pl.CostEstimate(flops=0, bytes_accessed=10 * 10**6, transcendentals=0),
    )(*outs)


def solution(mesh):
    return jax.shard_map(
        local,
        mesh=mesh,
        in_specs=(
            P(("wide", "narrow"), None),
            P(),
            P(("wide", "narrow"), None, None),
            P(("wide", "narrow"), None, None),
            P(("wide", "narrow"), None),
        ),
        out_specs=(
            P(("wide", "narrow"), None),
            P(),
            P(("wide", "narrow"), None, None),
            P(("wide", "narrow"), None, None),
        ),
        check_vma=False,
    )
```
